32 devices in a mesh: grp: 2 (over x), tile: 16 (over z, y, core).
Axes of the slice: x: 2, y: 2, z: 4, core: 2. Of those that a mesh axis runs over, the one named last changes fastest.
Arguments:
- starting_element_condition: bfloat16 [4096, 512], P(('grp', 'tile')), parts along dimension 0, may hold values from -6 to 6
- stored_lookup_record: bfloat16 [1, 4096, 512], P(None, ('grp', 'tile')), parts along dimension 1, may hold values from -6 to 6
- stored_content_record: bfloat16 [1, 4096, 512], P(None, ('grp', 'tile')), parts along dimension 1, may hold values from -6 to 6
- scaling_multiplier_entries: float32 [512], replicated, may hold values from 0.1 to 1.9
- joint_projector_coefficients: bfloat16 [512, 1536], replicated, may hold values from -0.25 to 0.25
- final_projector: bfloat16 [512, 512], replicated, may hold values from -0.25 to 0.25
- sharpness_factor: float32 [8], replicated, may hold values from 16 to 32
- adjacent_marine_connection: int32 [32, 8], P(('grp', 'tile')), parts along dimension 0, may hold values 0 or 1
- segment_marine_marks: int32 [256], P(('grp', 'tile')), parts along dimension 0, may hold values 0 or 1
- patch_element_amounts: int32 [32], P(('grp', 'tile')), parts along dimension 0, may hold values from 32 to 128, as said below
Outputs:
- tendencies: bfloat16 [2, 4096, 512], P(None, ('grp', 'tile')), parts along dimension 1
The draws below stay inside these ranges and needn't reach their ends.
There are 2 independent parts, one for each index of `grp`. The reference program is written for one: setup_inputs(seed, part) draws one part's arguments, and reference() takes and returns one part's arrays. A program takes and returns all parts, laid end to end along the dimension named above; an argument that names none is the same for every part. Nothing has to cross between parts.
Inputs may be any that keep to these rules, and one draw needn't show every extreme that they name: `adjacent_marine_connection`: 1 where the tile's water reaches the neighbour in that direction, in the order of the steps. `segment_marine_marks`: 1 for a block of sea tokens, 0 for land. `patch_element_amounts`: tokens from this position of a tile on are padding; some tile is full.
All inputs are finite; a program needn't handle non-finite values. No bound on the sum of `adjacent_marine_connection` on one device may be relied on, other than what follows from the above.
Results may differ from the reference program's by a relative error of at most 0.023.
Values may be sent and summed in bfloat16 or wider, within the bound.
A program may use at most 64 MiB of HBM per device.

```python
import math
import jax
import jax.numpy as jnp
from jax import lax

D = 512
FOCUS_GROUPS = 8
HIST = 1
STEPS = 2
TOK = 128
BLK = 16
TW = 8
TILES = 16
TOKENS = 2048
BLOCKS = 128


def draw_patch_element_amounts(key, part):
    first_key, second_key = jax.random.split(key, 2)
    drawn = jax.random.randint(first_key, (TILES,), TOK // 4, TOK + 1)
    shuffled = jax.random.permutation(second_key, TILES)
    drawn = drawn.at[shuffled[0]].set(TOK)
    drawn = drawn.at[shuffled[1]].set(TOK // 4)
    return drawn.astype(jnp.int32)


def with_ends(entries, key, low, largest):
    spot = [jax.random.randint(jax.random.fold_in(key, axis), (), 0, length) for axis, length in enumerate(entries.shape)]
    longest = entries.shape.index(max(entries.shape))
    next_to = spot[:longest] + [(spot[longest] + 1) % entries.shape[longest]] + spot[longest + 1:]
    return entries.at[tuple(spot)].set(low).at[tuple(next_to)].set(largest)


def block_levels(key, shape, cuts, least, largest):
    level = 1.0
    for dim, shards_of in cuts:
        heights = jax.random.uniform(jax.random.fold_in(jax.random.fold_in(key, 6), dim), (shards_of,), jnp.float32, least / len(cuts), largest / len(cuts))
        level = level * jnp.repeat(jnp.exp(heights), shape[dim] // shards_of).reshape((-1,) + (1,) * (len(shape) - 1 - dim))
    return level


def gaussian(stream_key, extent, scale, most, cuts=(), kind=jnp.bfloat16):
    level = block_levels(stream_key, extent, cuts, -0.22, 0.18) if cuts else 1.0
    values = jax.random.normal(stream_key, extent, jnp.float32) * scale * level
    return jnp.minimum(jnp.maximum(values, -most), most).astype(kind)


def setup_inputs(seed: int = 0, part: int = 0) -> dict:
    splits = jax.random.split(jax.random.key(seed), 11)
    part_splits = jax.random.split(jax.random.fold_in(splits[10], part), 11)
    starting_element_condition = gaussian(part_splits[0], (TOKENS, D), 1.0, 6.0, ((0, 16),))
    stored_lookup_record = gaussian(part_splits[1], (HIST, TOKENS, D), 1.0, 6.0, ((1, 16),))
    stored_content_record = gaussian(part_splits[2], (HIST, TOKENS, D), 1.0, 6.0, ((1, 16),))
    scaling_multiplier_entries = jnp.clip(1.0 + 0.18 * jax.random.normal(splits[3], (D,), jnp.float32), 0.1, 1.9)
    joint_projector_coefficients = gaussian(splits[4], (D, 3 * D), D ** -0.5, 0.25)
    final_projector = gaussian(splits[5], (D, D), D ** -0.5, 0.25)
    sharpness_factor = jnp.clip(jnp.exp(jax.random.uniform(splits[6], (FOCUS_GROUPS,), jnp.float32, math.log(16.0), math.log(32.0))), 16.0, 32.0)
    adjacent_marine_connection = with_ends((jax.random.randint(part_splits[7], (TILES, 8), 0, 4) < 3).astype(jnp.int32), jax.random.fold_in(part_splits[7], 1), 0, 1)
    segment_marine_marks = with_ends((jax.random.randint(part_splits[8], (BLOCKS,), 0, 4) < 3).astype(jnp.int32), jax.random.fold_in(part_splits[8], 1), 0, 1)
    patch_element_amounts = draw_patch_element_amounts(jax.random.fold_in(jax.random.fold_in(splits[10], part), 71), part)
    return dict(starting_element_condition=starting_element_condition, stored_lookup_record=stored_lookup_record, stored_content_record=stored_content_record, scaling_multiplier_entries=scaling_multiplier_entries, joint_projector_coefficients=joint_projector_coefficients, final_projector=final_projector, sharpness_factor=sharpness_factor, adjacent_marine_connection=adjacent_marine_connection, segment_marine_marks=segment_marine_marks, patch_element_amounts=patch_element_amounts)


DIRECTIONS = ((-1, -1), (-1, 0), (-1, 1), (0, -1), (0, 1), (1, -1), (1, 0), (1, 1))

def widen(array_in):
    return lax.optimization_barrier(array_in).astype(jnp.float32)

def unit_heads(array_in, group_quantity):
    dims = array_in.shape
    per_head = widen(array_in).reshape(dims[:-1] + (group_quantity, dims[-1] // group_quantity))
    inv_rms = lax.rsqrt(lax.optimization_barrier(jnp.mean(per_head * per_head, axis=-1, keepdims=True)) + 1e-06)
    return (per_head * inv_rms).reshape(dims).astype(jnp.bfloat16)

def plain_focus_pass(request_array, segment_lookup_entries, segment_content_entries, lookup_permitted, sharpness_factor):
    query_rows, model_width = request_array.shape
    group_quantity = sharpness_factor.shape[0]
    channel_dimension = model_width // group_quantity
    query_heads = widen(request_array).reshape(query_rows, group_quantity, channel_dimension)
    key_heads = widen(segment_lookup_entries).reshape(-1, group_quantity, channel_dimension)
    value_heads = widen(segment_content_entries).reshape(-1, group_quantity, channel_dimension)
    affinity_levels = jnp.einsum('qhd,khd->hqk', query_heads, key_heads)
    affinity_levels = affinity_levels * (sharpness_factor / channel_dimension)[:, None, None]
    weights = jnp.where(lookup_permitted[None, None, :], jnp.exp(affinity_levels), 0.0)
    denominator = lax.optimization_barrier(jnp.sum(weights, axis=-1)).T
    rounded = widen(weights.astype(jnp.bfloat16))
    numerator = jnp.einsum('hqk,khd->qhd', rounded, value_heads)
    return (numerator.reshape(query_rows, model_width), denominator)

def reference(starting_element_condition, stored_lookup_record, stored_content_record, scaling_multiplier_entries, joint_projector_coefficients, final_projector, sharpness_factor, adjacent_marine_connection, segment_marine_marks, patch_element_amounts):
    tile_total = TILES
    group_quantity = FOCUS_GROUPS
    window_len = HIST + 1
    grid_rows = tile_total // TW
    positions = jnp.arange(TOK, dtype=jnp.int32)
    spread = jnp.broadcast_to(segment_marine_marks.reshape(tile_total, TOK // BLK, 1), (tile_total, TOK // BLK, BLK)).reshape(tile_total, TOK)
    token_ok = (spread == 1) & (positions[None, :] < patch_element_amounts[:, None])
    tile_ids = jnp.arange(tile_total, dtype=jnp.int32)
    tile_row = tile_ids // TW
    tile_column = tile_ids % TW
    sources = [tile_ids]
    present = [jnp.ones((tile_total,), jnp.bool_)]
    for direction in range(8):
        row_delta, col_delta = DIRECTIONS[direction]
        near_row = tile_row + row_delta
        near_col = tile_column + col_delta
        inside = (near_row >= 0) & (near_row < grid_rows) & (near_col >= 0) & (near_col < TW)
        present.append(inside & (adjacent_marine_connection[:, direction] == 1))
        sources.append(jnp.clip(near_row * TW + near_col, 0, tile_total - 1).astype(jnp.int32))
    source_table = jnp.stack(sources, axis=1)
    present_table = jnp.stack(present, axis=1)
    spare_slots = jnp.zeros((STEPS, TOKENS, D), jnp.bfloat16)
    key_store = jnp.concatenate([unit_heads(stored_lookup_record, group_quantity), spare_slots], axis=0)
    value_store = jnp.concatenate([stored_content_record, spare_slots], axis=0)
    state_now = starting_element_condition
    results = []
    for step_index in range(STEPS):
        widened = widen(state_now)
        normed = (widened * lax.rsqrt(lax.optimization_barrier(jnp.mean(widened * widened, axis=-1, keepdims=True)) + 1e-06) * scaling_multiplier_entries).astype(jnp.bfloat16)
        projected = jnp.dot(normed, joint_projector_coefficients, preferred_element_type=jnp.float32).astype(jnp.bfloat16)
        request_array = unit_heads(projected[:, :D], group_quantity)
        new_keys = unit_heads(projected[:, D:2 * D], group_quantity)
        new_values = projected[:, 2 * D:]
        key_store = key_store.at[HIST + step_index].set(new_keys)
        value_store = value_store.at[HIST + step_index].set(new_values)
        window_keys = key_store[step_index:step_index + window_len].reshape(window_len, tile_total, TOK, D)
        window_values = value_store[step_index:step_index + window_len].reshape(window_len, tile_total, TOK, D)
        tile_queries = request_array.reshape(tile_total, TOK, D)

        def one_tile(tile_id):
            segment_request_entries = lax.dynamic_index_in_dim(tile_queries, tile_id, 0, keepdims=False)
            numerator = jnp.zeros((TOK, D), jnp.float32)
            denominator = jnp.zeros((TOK, group_quantity), jnp.float32)
            for source_slot in range(9):
                source = source_table[tile_id, source_slot]
                segment_lookup_entries = lax.dynamic_index_in_dim(window_keys, source, 1, keepdims=False).reshape(window_len * TOK, D)
                segment_content_entries = lax.dynamic_index_in_dim(window_values, source, 1, keepdims=False).reshape(window_len * TOK, D)
                source_ok = lax.dynamic_index_in_dim(token_ok, source, 0, keepdims=False)
                lookup_permitted = jnp.tile(source_ok, window_len) & present_table[tile_id, source_slot]
                running_weighted_sum, running_normalizer = plain_focus_pass(segment_request_entries, segment_lookup_entries, segment_content_entries, lookup_permitted, sharpness_factor)
                numerator = numerator + running_weighted_sum
                denominator = denominator + running_normalizer
            query_ok = lax.dynamic_index_in_dim(token_ok, tile_id, 0, keepdims=False)
            safe_total = jnp.where(query_ok[:, None], denominator, 1.0)
            attended = numerator.reshape(TOK, group_quantity, D // group_quantity) / safe_total[:, :, None]
            return jnp.where(query_ok[:, None, None], attended, 0.0).reshape(TOK, D)
        attended = lax.map(one_tile, tile_ids).reshape(TOKENS, D).astype(jnp.bfloat16)
        tendency = jnp.dot(attended, final_projector, preferred_element_type=jnp.float32).astype(jnp.bfloat16)
        state_now = (widen(state_now) + widen(tendency)).astype(jnp.bfloat16)
        results.append(tendency)
    return jnp.stack(results)
```

```python
import functools

import jax
import jax.numpy as jnp
from jax import lax
from jax.experimental import pallas as pl
from jax.experimental.pallas import tpu as pltpu
from jax.sharding import PartitionSpec as P

TW = 8
STEPS = 2
LOG2E = 1.4426950408889634
NT = (((1,), (1,)), ((), ()))
DIRECTIONS = ((-1, -1), (-1, 0), (-1, 1), (0, -1), (0, 1), (1, -1), (1, 0), (1, 1))


def dot(a, b):
    return jnp.dot(a, b, preferred_element_type=jnp.float32)


def kernel(
    tiles,
    x_ref,
    k_ref,
    v_ref,
    gain_ref,
    w_ref,
    wo_ref,
    sharp_ref,
    adj_ref,
    marks_ref,
    amount_ref,
    out_ref,
    gx,
    gk,
    gv,
    gx1,
    ks,
    vs,
    ms,
    qs,
    acc,
    ones_s,
    send_v,
    recv_v,
    send_h,
    recv_h,
):
    tok, width = x_ref.shape
    heads = sharp_ref.shape[0]
    hd = width // heads
    rows = tiles // TW
    t = lax.axis_index("tile")
    row = t // TW
    col = t % TW
    two = rows == 2
    groups = 2 if two else 3
    has_left = col > 0
    has_right = col < TW - 1
    if two:
        verticals = [(1, 1, None, jnp.where(row == 0, t + TW, t - TW))]
    else:
        verticals = [
            (1, 2, row > 0, jnp.maximum(t - TW, 0)),
            (2, 1, row < rows - 1, jnp.minimum(t + TW, tiles - 1)),
        ]
    sides = [
        (has_right, jnp.minimum(t + 1, tiles - 1), has_left),
        (has_left, jnp.maximum(t - 1, 0), has_right),
    ]
    group_on = [None] + [v[2] for v in verticals]

    def when(*conds):
        conds = [c for c in conds if c is not None]
        if not conds:
            return lambda f: f()
        c = conds[0]
        for d in conds[1:]:
            c = jnp.logical_and(c, d)
        return pl.when(c)

    bufs = [gx, gk, gv, gx1]

    def vcopy(chunk, i):
        here, there, _, dev = verticals[i]
        return pltpu.make_async_remote_copy(
            src_ref=bufs[chunk].at[0, 0],
            dst_ref=bufs[chunk].at[there, 0],
            send_sem=send_v.at[chunk, there],
            recv_sem=recv_v.at[chunk, there],
            device_id={"tile": dev},
            device_id_type=pl.DeviceIdType.MESH,
        )

    def vwait(chunk, i):
        here, _, _, dev = verticals[i]
        pltpu.make_async_remote_copy(
            src_ref=bufs[chunk].at[0, 0],
            dst_ref=bufs[chunk].at[here, 0],
            send_sem=send_v.at[chunk, here],
            recv_sem=recv_v.at[chunk, here],
            device_id={"tile": dev},
            device_id_type=pl.DeviceIdType.MESH,
        ).wait_recv()

    def hcopy(chunk, g, side):
        return pltpu.make_async_remote_copy(
            src_ref=bufs[chunk].at[g, 0],
            dst_ref=bufs[chunk].at[g, 1 + side],
            send_sem=send_h.at[chunk, g, side],
            recv_sem=recv_h.at[chunk, g, side],
            device_id={"tile": sides[side][1]},
            device_id_type=pl.DeviceIdType.MESH,
        )

    barrier = pltpu.get_barrier_semaphore()
    reach = [(v[2], v[3]) for v in verticals] + [(s[0], s[1]) for s in sides]
    for on, dev in reach:

        @when(on)
        def _(dev=dev):
            pl.semaphore_signal(
                barrier, inc=1, device_id={"tile": dev}, device_id_type=pl.DeviceIdType.MESH
            )

    blocks = marks_ref.shape[0]
    per = tok // blocks

    def validity(pos):
        m = jnp.zeros(pos.shape, jnp.int32)
        for b in range(blocks):
            m = jnp.where((pos >= b * per) & (pos < (b + 1) * per), marks_ref[b], m)
        return (m == 1) & (pos < amount_ref[0])

    ri = lax.broadcasted_iota(jnp.int32, (tok, tok), 0)
    ci = lax.broadcasted_iota(jnp.int32, (tok, tok), 1)
    ok = validity(ri)
    gx[0, 0, :tok, :] = x_ref[...]
    gx[0, 0, tok:, :] = jnp.zeros((16, width), jnp.bfloat16)
    gx[0, 0, tok:, :tok] = jnp.where(
        validity(lax.broadcasted_iota(jnp.int32, (16, tok), 1)), 1.0, 0.0
    ).astype(jnp.bfloat16)
    gv[0, 0] = v_ref[0]
    qw = 4 * hd
    e0 = lax.broadcasted_iota(jnp.int32, (qw, qw), 0) >> 6
    e1 = lax.broadcasted_iota(jnp.int32, (qw, qw), 1) >> 6
    ones_s[...] = jnp.where(e0 == e1, 1.0 / hd, 0.0).astype(jnp.bfloat16)

    peers = 0
    for on, dev in reach:
        peers = peers + (1 if on is None else on.astype(jnp.int32))
    pl.semaphore_wait(barrier, peers)

    def start_vertical(chunk):
        for i, v in enumerate(verticals):

            @when(v[2])
            def _(i=i):
                vcopy(chunk, i).start()

    def start_sides(chunk, g):
        for side in range(2):

            @when(sides[side][0], group_on[g])
            def _(side=side):
                hcopy(chunk, g, side).start()

    def unit(u):
        f = u.astype(jnp.float32)
        sq = (f * f).astype(jnp.bfloat16)
        mean = jnp.concatenate(
            [dot(sq[:, i : i + qw], ones_s[...]) for i in range(0, width, qw)], axis=1
        )
        return f * lax.rsqrt(mean + 1e-06)

    start_vertical(0)
    start_vertical(2)
    start_sides(0, 0)
    start_sides(2, 0)
    gk[0, 0] = unit(k_ref[0]).astype(jnp.bfloat16)
    start_vertical(1)
    start_sides(1, 0)

    lane = lax.broadcasted_iota(jnp.int32, (1, width), 1)
    scale = jnp.zeros((1, width), jnp.float32)
    for h in range(heads):
        scale = jnp.where(
            (lane >= h * hd) & (lane < (h + 1) * hd), sharp_ref[h] * (LOG2E / hd), scale
        )

    def norm(x):
        f = x.astype(jnp.float32)
        r = lax.rsqrt(jnp.mean(f * f, axis=-1, keepdims=True) + 1e-06)
        return (f * r * gain_ref[...]).astype(jnp.bfloat16)

    def slot_of(g, c):
        return g * 3 + c

    def present(g, c):
        dc = (0, -1, 1)[c]

        def adj(dr):
            return adj_ref[0, DIRECTIONS.index((dr, dc))]

        if g == 0:
            return None if c == 0 else adj(0)
        if two:
            return jnp.where(row == 0, adj(1), adj(-1))
        return adj(-1) if g == 1 else adj(1)

    quads = width // qw

    def attend(s, g, c, first):
        n = slot_of(g, c)
        m = ms[n]
        for q in range(quads):
            keys = ks[n, s * tok : (s + 2) * tok, q * qw : (q + 1) * qw]
            scores = lax.dot_general(qs[q], keys, NT, preferred_element_type=jnp.float32)
            p = jnp.exp2(scores).astype(jnp.bfloat16)
            for a in range(2):
                pair = q * 2 + a
                vals = vs[n, s * tok : (s + 2) * tok, pair * 2 * hd : (pair + 1) * 2 * hd]
                r = dot(p[a * 2 * tok : (a + 1) * 2 * tok], jnp.concatenate([vals, m], axis=1))
                if first:
                    acc[pair] = r
                else:
                    acc[pair] += r

    def project(s, g, c, x):
        n = slot_of(g, c)
        kv = dot(norm(x), w_ref[:, width:]).astype(jnp.bfloat16)
        base = (s + 1) * tok
        ks[n, base : base + tok, :] = unit(kv[:, :width]).astype(jnp.bfloat16)
        m = ms[n, :tok, :1].astype(jnp.float32)
        vs[n, base : base + tok, :] = (kv[:, width:].astype(jnp.float32) * m).astype(
            jnp.bfloat16
        )

    def prepare(g, c):
        n = slot_of(g, c)
        line = gx[g, c, tok : tok + 16, :tok].astype(jnp.float32)[:1]
        m = jnp.sum(jnp.where(ri == ci, line, 0.0), axis=1, keepdims=True)
        seen = present(g, c)
        if seen is not None:
            m = m * jnp.where(seen == 1, 1.0, 0.0)
        mb = jnp.broadcast_to(m, (tok, 2 * hd)).astype(jnp.bfloat16)
        ms[n, :tok, :] = mb
        ms[n, tok:, :] = mb
        ks[n, :tok, :] = gk[g, c]
        vs[n, :tok, :] = (gv[g, c].astype(jnp.float32) * m).astype(jnp.bfloat16)

    def source(s, g, c, first=False):
        if s == 0:
            prepare(g, c)
            project(s, g, c, gx[g, c, :tok, :])
        else:
            project(s, g, c, gx1[g, c])
        attend(s, g, c, first)

    for s in range(STEPS):
        chunks = (0, 2, 1) if s == 0 else (3,)
        x = x_ref[...] if s == 0 else gx1[0, 0]
        if s == 1:
            start_vertical(3)
            start_sides(3, 0)
        u = dot(norm(x), w_ref[:, :width]).astype(jnp.bfloat16)
        query = unit(u) * scale
        for q in range(quads):
            part = query[:, q * qw : (q + 1) * qw]
            lanes = lax.broadcasted_iota(jnp.int32, (tok, qw), 1)
            for a in range(4):
                qs[q, a * tok : (a + 1) * tok, :] = jnp.where(
                    (lanes >= a * hd) & (lanes < (a + 1) * hd), part, 0.0
                ).astype(jnp.bfloat16)
        source(s, 0, 0, True)

        def from_side(g, side):
            @when(sides[side][2], group_on[g])
            def _():
                for chunk in chunks:
                    hcopy(chunk, g, side).wait_recv()
                source(s, g, 1 + side)

        from_side(0, 0)
        from_side(0, 1)
        for i, v in enumerate(verticals):
            g = v[0]
            for chunk in chunks:

                @when(v[2])
                def _(chunk=chunk, i=i):
                    vwait(chunk, i)

                start_sides(chunk, g)

            @when(v[2])
            def _(g=g):
                source(s, g, 0)

        for v in verticals:
            from_side(v[0], 0)
            from_side(v[0], 1)
        half = lax.broadcasted_iota(jnp.int32, (tok, 2 * hd), 1) < hd
        outs = []
        for pair in range(heads // 2):
            top = acc[pair, :tok, :]
            bot = acc[pair, tok:, :]
            num = jnp.where(half, top[:, : 2 * hd], bot[:, : 2 * hd])
            den = jnp.where(half, top[:, 2 * hd :], bot[:, 2 * hd :])
            outs.append(
                jnp.where(ok, num / jnp.where(ok, den, 1.0), 0.0).astype(jnp.bfloat16)
            )
        tend = dot(jnp.concatenate(outs, axis=1), wo_ref[...]).astype(jnp.bfloat16)
        out_ref[s] = tend
        if s == 0:
            gx1[0, 0] = (x.astype(jnp.float32) + tend.astype(jnp.float32)).astype(jnp.bfloat16)

    for chunk in range(4):
        for i, v in enumerate(verticals):

            @when(v[2])
            def _(i=i):
                vcopy(chunk, i).wait_send()

        for g in range(groups):
            for side in range(2):

                @when(sides[side][0], group_on[g])
                def _(g=g, side=side):
                    hcopy(chunk, g, side).wait_send()


def body(tiles, x, k, v, gain, w, wo, sharp, adj, marks, amount):
    tok, width = x.shape
    groups = 2 if tiles // TW == 2 else 3
    slots = 3 * groups
    vmem = pl.BlockSpec(memory_space=pltpu.VMEM)
    smem = pl.BlockSpec(memory_space=pltpu.SMEM)
    bf = jnp.bfloat16
    hd = width // sharp.shape[0]
    return pl.pallas_call(
        functools.partial(kernel, tiles),
        out_shape=jax.ShapeDtypeStruct((STEPS, tok, width), bf),
        in_specs=[vmem] * 6 + [smem] * 4,
        out_specs=vmem,
        scratch_shapes=[
            pltpu.VMEM((groups, 3, tok + 16, width), bf),
            pltpu.VMEM((groups, 3, tok, width), bf),
            pltpu.VMEM((groups, 3, tok, width), bf),
            pltpu.VMEM((groups, 3, tok, width), bf),
            pltpu.VMEM((slots, 3 * tok, width), bf),
            pltpu.VMEM((slots, 3 * tok, width), bf),
            pltpu.VMEM((slots, 2 * tok, 2 * hd), bf),
            pltpu.VMEM((width // (4 * hd), 4 * tok, 4 * hd), bf),
            pltpu.VMEM((width // (2 * hd), 2 * tok, 4 * hd), jnp.float32),
            pltpu.VMEM((4 * hd, 4 * hd), bf),
            pltpu.SemaphoreType.DMA((4, 3)),
            pltpu.SemaphoreType.DMA((4, 3)),
            pltpu.SemaphoreType.DMA((4, 3, 2)),
            pltpu.SemaphoreType.DMA((4, 3, 2)),
        ],
        compiler_params=pltpu.CompilerParams(
            collective_id=0, has_side_effects=True, vmem_limit_bytes=48 * 1024 * 1024
        ),
    )(x, k, v, gain.reshape(1, width), w, wo, sharp, adj, marks, amount)


def solution(mesh):
    part = ("grp", "tile")
    in_specs = (
        P(part, None),
        P(None, part, None),
        P(None, part, None),
        P(),
        P(),
        P(),
        P(),
        P(part, None),
        P(part),
        P(part),
    )
    return jax.shard_map(
        functools.partial(body, mesh.shape["tile"]),
        mesh=mesh,
        in_specs=in_specs,
        out_specs=P(None, part, None),
        check_vma=False,
    )
```

```python
import functools

import jax
import jax.numpy as jnp
from jax import lax
from jax.experimental import pallas as pl
from jax.experimental.pallas import tpu as pltpu
from jax.sharding import PartitionSpec as P

TW = 8
STEPS = 2
COLS = (0, -1, 1)
LOG2E = 1.4426950408889634
NT = (((1,), (1,)), ((), ()))
DIRECTIONS = ((-1, -1), (-1, 0), (-1, 1), (0, -1), (0, 1), (1, -1), (1, 0), (1, 1))


def dot(a, b):
    return jnp.dot(a, b, preferred_element_type=jnp.float32)


def kernel(
    tiles,
    x_hbm,
    k_hbm,
    v_hbm,
    gain_hbm,
    w_hbm,
    wo_hbm,
    sharp_hbm,
    adj_hbm,
    marks_hbm,
    amount_hbm,
    out_ref,
    k_ref,
    gain_ref,
    w_ref,
    wo_ref,
    sharp_ref,
    adj_ref,
    marks_ref,
    amount_ref,
    local,
    gx,
    gk,
    gv,
    ks,
    vs,
    ms,
    qs,
    nums,
    dens,
    psend,
    precv,
    ones_s,
    send_v,
    recv_v,
    send_h,
    recv_h,
    send_p,
    recv_p,
):
    tok, width = x_hbm.shape
    heads = sharp_hbm.shape[0]
    hd = width // heads
    qw = 4 * hd
    quads = width // qw
    rows = tiles // TW
    t = lax.axis_index("tile")
    row = t // TW
    col = t % TW
    two = rows == 2
    has_left = col > 0
    has_right = col < TW - 1
    if two:
        verticals = [(0, 0, None, jnp.where(row == 0, t + TW, t - TW))]
    else:
        verticals = [
            (0, 1, row > 0, jnp.maximum(t - TW, 0)),
            (1, 0, row < rows - 1, jnp.minimum(t + TW, tiles - 1)),
        ]
    sides = [
        (has_right, jnp.minimum(t + 1, tiles - 1), has_left),
        (has_left, jnp.maximum(t - 1, 0), has_right),
    ]

    def when(cond):
        return (lambda f: f()) if cond is None else pl.when(cond)

    def place(chunk, slot):
        if chunk == 0:
            return gx.at[0, slot]
        if chunk == 3:
            return gx.at[1, slot, :tok]
        return (gk if chunk == 1 else gv).at[slot]

    def remote(src, dst, send, recv, dev):
        return pltpu.make_async_remote_copy(
            src_ref=src,
            dst_ref=dst,
            send_sem=send,
            recv_sem=recv,
            device_id={"tile": dev},
            device_id_type=pl.DeviceIdType.MESH,
        )

    def vcopy(chunk, at, dev):
        c = chunk // 3
        return remote(
            place(chunk, 0), place(chunk, 3 + at), send_v.at[c, at], recv_v.at[c, at], dev
        )

    def hcopy(chunk, side):
        return remote(
            place(chunk, 0),
            place(chunk, 1 + side),
            send_h.at[chunk, side],
            recv_h.at[chunk, side],
            sides[side][1],
        )

    def pcopy(s, src, dst, q, dev):
        return remote(
            psend.at[s, src, q],
            precv.at[s, dst, q],
            send_p.at[s, dst, q],
            recv_p.at[s, dst, q],
            dev,
        )

    barrier = pltpu.get_barrier_semaphore()
    reach = [(v[2], v[3]) for v in verticals] + [(s[0], s[1]) for s in sides]
    for on, dev in reach:

        @when(on)
        def _(dev=dev):
            pl.semaphore_signal(
                barrier, inc=1, device_id={"tile": dev}, device_id_type=pl.DeviceIdType.MESH
            )

    loads = [
        (marks_hbm, marks_ref),
        (amount_hbm, amount_ref),
        (adj_hbm, adj_ref),
        (x_hbm, gx.at[0, 0, :tok]),
        (v_hbm.at[0], gv.at[0]),
        (k_hbm, k_ref),
        (gain_hbm, gain_ref),
        (w_hbm, w_ref),
        (sharp_hbm, sharp_ref),
        (wo_hbm, wo_ref),
    ]
    loads = [pltpu.make_async_copy(a, b, local.at[i]) for i, (a, b) in enumerate(loads)]
    for load in loads:
        load.start()
    blocks = marks_ref.shape[0]
    per = tok // blocks

    def validity(pos):
        m = jnp.zeros(pos.shape, jnp.int32)
        for b in range(blocks):
            m = jnp.where((pos >= b * per) & (pos < (b + 1) * per), marks_ref[b], m)
        return (m == 1) & (pos < amount_ref[0])

    ri = lax.broadcasted_iota(jnp.int32, (tok, tok), 0)
    ci = lax.broadcasted_iota(jnp.int32, (tok, tok), 1)
    loads[0].wait()
    loads[1].wait()
    loads[2].wait()
    ok = validity(ri)
    up8 = lax.broadcasted_iota(jnp.int32, (16, tok), 0) < 8
    for c, dc in enumerate(COLS):
        up = adj_ref[0, DIRECTIONS.index((-1, dc))]
        down = adj_ref[0, DIRECTIONS.index((1, dc))]
        gx[0, 0, tok:, (c + 1) * tok : (c + 2) * tok] = jnp.where(
            jnp.where(up8, up, down) == 1, 1.0, 0.0
        ).astype(jnp.bfloat16)
    gx[0, 0, tok:, :tok] = jnp.where(
        validity(lax.broadcasted_iota(jnp.int32, (16, tok), 1)), 1.0, 0.0
    ).astype(jnp.bfloat16)
    e0 = lax.broadcasted_iota(jnp.int32, (qw, qw), 0) >> 6
    e1 = lax.broadcasted_iota(jnp.int32, (qw, qw), 1) >> 6
    ones_s[...] = jnp.where(e0 == e1, 1.0 / hd, 0.0).astype(jnp.bfloat16)

    peers = 0
    for on, dev in reach:
        peers = peers + (1 if on is None else on.astype(jnp.int32))
    pl.semaphore_wait(barrier, peers)

    def start_vertical(chunk):
        for _, there, on, dev in verticals:

            @when(on)
            def _(there=there, dev=dev):
                vcopy(chunk, there, dev).start()

    def start_sides(chunk):
        for side in range(2):

            @when(sides[side][0])
            def _(side=side):
                hcopy(chunk, side).start()

    def unit(u):
        f = u.astype(jnp.float32)
        sq = (f * f).astype(jnp.bfloat16)
        mean = jnp.concatenate(
            [dot(sq[:, i : i + qw], ones_s[...]) for i in range(0, width, qw)], axis=1
        )
        return f * lax.rsqrt(mean + 1e-06)

    loads[3].wait()
    start_vertical(0)
    start_sides(0)
    loads[4].wait()
    start_sides(2)
    loads[5].wait()
    gk[0] = unit(k_ref[0]).astype(jnp.bfloat16)
    start_sides(1)

    for load in loads[6:]:
        load.wait()
    lane = lax.broadcasted_iota(jnp.int32, (1, width), 1)
    scale = jnp.zeros((1, width), jnp.float32)
    for h in range(heads):
        scale = jnp.where(
            (lane >= h * hd) & (lane < (h + 1) * hd), sharp_ref[h] * (LOG2E / hd), scale
        )
    hrow = lax.broadcasted_iota(jnp.int32, (16, qw), 0)
    hlane = lax.broadcasted_iota(jnp.int32, (16, qw), 1)
    pick = jnp.where(hlane == hrow * hd, 1.0, 0.0).astype(jnp.bfloat16)
    spread = jnp.where(
        (hlane >= hrow * hd) & (hlane < (hrow + 1) * hd), 1.0, 0.0
    ).astype(jnp.bfloat16)
    half = lax.broadcasted_iota(jnp.int32, (tok, 2 * hd), 1) < hd

    for side in range(2):

        @pl.when(jnp.logical_not(sides[side][2]))
        def _(n=1 + side):
            ks[n] = jnp.zeros(ks.shape[1:], jnp.bfloat16)
            vs[n] = jnp.zeros(vs.shape[1:], jnp.bfloat16)
            ms[n] = jnp.zeros(ms.shape[1:], jnp.bfloat16)

    def norm(x):
        f = x.astype(jnp.float32)
        r = lax.rsqrt(jnp.mean(f * f, axis=-1, keepdims=True) + 1e-06)
        return (f * r * gain_ref[...]).astype(jnp.bfloat16)

    def make_query(i, x):
        u = dot(norm(x), w_ref[:, :width]).astype(jnp.bfloat16)
        query = unit(u) * scale
        for q in range(quads):
            part = query[:, q * qw : (q + 1) * qw]
            lanes = lax.broadcasted_iota(jnp.int32, (tok, qw), 1)
            for a in range(4):
                qs[i, q, a * tok : (a + 1) * tok, :] = jnp.where(
                    (lanes >= a * hd) & (lanes < (a + 1) * hd), part, 0.0
                ).astype(jnp.bfloat16)

    def prepare(n):
        line = gx[0, n, tok:, :tok].astype(jnp.float32)[:1]
        m = jnp.sum(jnp.where(ri == ci, line, 0.0), axis=1, keepdims=True)
        mb = jnp.broadcast_to(m, (tok, 2 * hd)).astype(jnp.bfloat16)
        ms[n, :tok, :] = mb
        ms[n, tok:, :] = mb
        ks[n, :tok, :] = gk[n]
        vs[n, :tok, :] = (gv[n].astype(jnp.float32) * m).astype(jnp.bfloat16)

    def project(s, n):
        kv = dot(norm(gx[s, n, :tok, :]), w_ref[:, width:]).astype(jnp.bfloat16)
        base = (s + 1) * tok
        ks[n, base : base + tok, :] = unit(kv[:, :width]).astype(jnp.bfloat16)
        m = ms[n, :tok, :1].astype(jnp.float32)
        vs[n, base : base + tok, :] = (kv[:, width:].astype(jnp.float32) * m).astype(
            jnp.bfloat16
        )

    def attend(s, i, q, seen):
        sums = [None, None]
        for c in range(3):
            keys = ks[c, s * tok : (s + 2) * tok, q * qw : (q + 1) * qw]
            scores = lax.dot_general(qs[i, q], keys, NT, preferred_element_type=jnp.float32)
            p = jnp.exp2(scores).astype(jnp.bfloat16)
            for a in range(2):
                lo = (q * 2 + a) * 2 * hd
                vals = vs[c, s * tok : (s + 2) * tok, lo : lo + 2 * hd]
                r = dot(p[a * 2 * tok : (a + 1) * 2 * tok], jnp.concatenate([vals, ms[c]], axis=1))
                if seen[c] is not None:
                    r = r * seen[c]
                sums[a] = r if sums[a] is None else sums[a] + r
        num, den = [], []
        for r in sums:
            top, bot = r[:tok], r[tok:]
            num.append(jnp.where(half, top[:, : 2 * hd], bot[:, : 2 * hd]))
            den.append(jnp.where(half, top[:, 2 * hd :], bot[:, 2 * hd :]))
        return jnp.concatenate(num, axis=1), jnp.concatenate(den, axis=1)

    own_seen = [None]
    for dc in (-1, 1):
        own_seen.append(jnp.where(adj_ref[0, DIRECTIONS.index((0, dc))] == 1, 1.0, 0.0))

    for s in range(STEPS):
        if s > 0:
            start_vertical(3)
            start_sides(3)
        make_query(0, gx[s, 0, :tok, :])
        if s == 0:
            prepare(0)
        project(s, 0)
        for here, _, on, dev in verticals:

            @when(on)
            def _(here=here, dev=dev):
                vcopy(3 * s, here, dev).wait_recv()
                make_query(1 + here, gx[s, 3 + here, :tok, :])

        for side in range(2):

            @pl.when(sides[side][2])
            def _(side=side):
                for chunk in (0, 2, 1) if s == 0 else (3,):
                    hcopy(chunk, side).wait_recv()
                if s == 0:
                    prepare(1 + side)
                project(s, 1 + side)

        for here, there, on, dev in verticals:

            @when(on)
            def _(here=here, there=there, dev=dev):
                lines = gx[0, 3 + here, tok:, :].astype(jnp.float32)
                up, down = lines[:1], lines[8:9]
                if two:
                    line = jnp.where(row == 0, up, down)
                else:
                    line = down if here == 0 else up
                seen = []
                for c, dc in enumerate(COLS):
                    part = line[:, (c + 1) * tok : (c + 2) * tok]
                    seen.append(jnp.concatenate([part] * (qw // tok), axis=1))
                for q in range(quads):
                    num, den = attend(s, 1 + here, q, seen)
                    psend[s, here, q, :tok, :] = num.astype(jnp.bfloat16)
                    low = lax.dot_general(
                        pick, den.astype(jnp.bfloat16), NT, preferred_element_type=jnp.float32
                    ).astype(jnp.bfloat16)
                    psend[s, here, q, tok:, :] = jnp.concatenate([low] * (qw // tok), axis=1)
                    pcopy(s, here, there, q, dev).start()

        for q in range(quads):
            nums[q], dens[q] = attend(s, 0, q, own_seen)
        for here, _, on, dev in verticals:
            for q in range(quads):

                @when(on)
                def _(here=here, dev=dev, q=q):
                    pcopy(s, here, here, q, dev).wait_recv()
                    nums[q] += precv[s, here, q, :tok, :].astype(jnp.float32)
                    dens[q] += lax.dot_general(
                        precv[s, here, q, tok:, :tok],
                        spread,
                        (((0,), (0,)), ((), ())),
                        preferred_element_type=jnp.float32,
                    )

        valid = jnp.concatenate([ok] * (qw // tok), axis=1)
        outs = [
            jnp.where(valid, nums[q] / jnp.where(valid, dens[q], 1.0), 0.0).astype(jnp.bfloat16)
            for q in range(quads)
        ]
        tend = dot(jnp.concatenate(outs, axis=1), wo_ref[...]).astype(jnp.bfloat16)
        if s == 0:
            x = gx[0, 0, :tok, :].astype(jnp.float32)
            gx[1, 0, :tok, :] = (x + tend.astype(jnp.float32)).astype(jnp.bfloat16)
        out_ref[s] = tend

    for here, there, on, dev in verticals:

        @when(on)
        def _(here=here, there=there, dev=dev):
            for s in range(STEPS):
                vcopy(3 * s, there, dev).wait_send()
                for q in range(quads):
                    pcopy(s, here, there, q, dev).wait_send()

    for side in range(2):

        @pl.when(sides[side][0])
        def _(side=side):
            for chunk in range(4):
                hcopy(chunk, side).wait_send()


def body(tiles, x, k, v, gain, w, wo, sharp, adj, marks, amount):
    tok, width = x.shape
    nv = 1 if tiles // TW == 2 else 2
    vmem = pl.BlockSpec(memory_space=pltpu.VMEM)
    hbm = pl.BlockSpec(memory_space=pltpu.HBM)
    bf = jnp.bfloat16
    hd = width // sharp.shape[0]
    qw = 4 * hd
    quads = width // qw
    return pl.pallas_call(
        functools.partial(kernel, tiles),
        out_shape=jax.ShapeDtypeStruct((STEPS, tok, width), bf),
        in_specs=[hbm] * 10,
        out_specs=vmem,
        scratch_shapes=[
            pltpu.VMEM(k.shape, bf),
            pltpu.VMEM((1, width), jnp.float32),
            pltpu.VMEM(w.shape, bf),
            pltpu.VMEM(wo.shape, bf),
            pltpu.SMEM(sharp.shape, jnp.float32),
            pltpu.SMEM(adj.shape, jnp.int32),
            pltpu.SMEM(marks.shape, jnp.int32),
            pltpu.SMEM(amount.shape, jnp.int32),
            pltpu.SemaphoreType.DMA((10,)),
            pltpu.VMEM((STEPS, 3 + nv, tok + 16, width), bf),
            pltpu.VMEM((3, tok, width), bf),
            pltpu.VMEM((3, tok, width), bf),
            pltpu.VMEM((3, 3 * tok, width), bf),
            pltpu.VMEM((3, 3 * tok, width), bf),
            pltpu.VMEM((3, 2 * tok, 2 * hd), bf),
            pltpu.VMEM((1 + nv, quads, 4 * tok, qw), bf),
            pltpu.VMEM((quads, tok, qw), jnp.float32),
            pltpu.VMEM((quads, tok, qw), jnp.float32),
            pltpu.VMEM((STEPS, nv, quads, tok + 16, qw), bf),
            pltpu.VMEM((STEPS, nv, quads, tok + 16, qw), bf),
            pltpu.VMEM((qw, qw), bf),
            pltpu.SemaphoreType.DMA((STEPS, nv)),
            pltpu.SemaphoreType.DMA((STEPS, nv)),
            pltpu.SemaphoreType.DMA((4, 2)),
            pltpu.SemaphoreType.DMA((4, 2)),
            pltpu.SemaphoreType.DMA((STEPS, nv, quads)),
            pltpu.SemaphoreType.DMA((STEPS, nv, quads)),
        ],
        compiler_params=pltpu.CompilerParams(
            collective_id=0, has_side_effects=True, vmem_limit_bytes=62 * 1024 * 1024
        ),
    )(x, k, v, gain.reshape(1, width), w, wo, sharp, adj, marks, amount)


def solution(mesh):
    part = ("grp", "tile")
    in_specs = (
        P(part, None),
        P(None, part, None),
        P(None, part, None),
        P(),
        P(),
        P(),
        P(),
        P(part, None),
        P(part),
        P(part),
    )
    return jax.shard_map(
        functools.partial(body, mesh.shape["tile"]),
        mesh=mesh,
        in_specs=in_specs,
        out_specs=P(None, part, None),
        check_vma=False,
    )
```

```python
import functools

import jax
import jax.numpy as jnp
from jax import lax
from jax.experimental import pallas as pl
from jax.experimental.pallas import tpu as pltpu
from jax.sharding import PartitionSpec as P

TW = 8
STEPS = 2
COLS = (0, -1, 1)
LOG2E = 1.4426950408889634
NT = (((1,), (1,)), ((), ()))
DIRECTIONS = ((-1, -1), (-1, 0), (-1, 1), (0, -1), (0, 1), (1, -1), (1, 0), (1, 1))


def dot(a, b):
    return jnp.dot(a, b, preferred_element_type=jnp.float32)


def kernel(
    tiles,
    x_hbm,
    k_hbm,
    v_hbm,
    gain_hbm,
    w_hbm,
    wo_hbm,
    sharp_hbm,
    adj_hbm,
    marks_hbm,
    amount_hbm,
    out_ref,
    k_ref,
    gain_ref,
    w_ref,
    wo_ref,
    sharp_ref,
    adj_ref,
    marks_ref,
    amount_ref,
    local,
    gx,
    gk,
    gv,
    ks,
    vs,
    ms,
    qs,
    nums,
    dens,
    psend,
    precv,
    lsend,
    lrecv,
    ones_s,
    send_v,
    recv_v,
    send_h,
    recv_h,
    send_p,
    recv_p,
):
    tok, width = x_hbm.shape
    heads = sharp_hbm.shape[0]
    hd = width // heads
    qw = 4 * hd
    quads = width // qw
    ht = tok // 2
    base = 16
    rows = tiles // TW
    t = lax.axis_index("tile")
    row = t // TW
    col = t % TW
    two = rows == 2
    has_left = col > 0
    has_right = col < TW - 1
    if two:
        verticals = [(0, 0, None, jnp.where(row == 0, t + TW, t - TW))]
    else:
        verticals = [
            (0, 1, row > 0, jnp.maximum(t - TW, 0)),
            (1, 0, row < rows - 1, jnp.minimum(t + TW, tiles - 1)),
        ]
    sides = [
        (has_right, jnp.minimum(t + 1, tiles - 1), has_left),
        (has_left, jnp.maximum(t - 1, 0), has_right),
    ]

    def when(cond):
        return (lambda f: f()) if cond is None else pl.when(cond)

    def place(chunk, slot):
        if chunk == 0:
            return gx.at[0, slot]
        if chunk >= 3:
            lo = base + (chunk - 3) * ht
            return gx.at[1, slot, lo : lo + ht]
        return (gk if chunk == 1 else gv).at[slot]

    def remote(src, dst, send, recv, dev):
        return pltpu.make_async_remote_copy(
            src_ref=src,
            dst_ref=dst,
            send_sem=send,
            recv_sem=recv,
            device_id={"tile": dev},
            device_id_type=pl.DeviceIdType.MESH,
        )

    def vcopy(s, h, at, dev):
        lo = 0 if s == 0 and h == 0 else base + h * ht
        hi = base + (h + 1) * ht
        return remote(
            gx.at[s, 0, lo:hi],
            gx.at[s, 3 + at, lo:hi],
            send_v.at[s, h, at],
            recv_v.at[s, h, at],
            dev,
        )

    def hcopy(chunk, side):
        return remote(
            place(chunk, 0),
            place(chunk, 1 + side),
            send_h.at[chunk, side],
            recv_h.at[chunk, side],
            sides[side][1],
        )

    def pcopies(s, src, dst, h, dev):
        return [
            remote(a.at[s, src, h], b.at[s, dst, h], send_p.at[s, dst, k], recv_p.at[s, dst, k], dev)
            for k, a, b in ((2 * h, lsend, lrecv), (2 * h + 1, psend, precv))
        ]

    barrier = pltpu.get_barrier_semaphore()
    reach = [(v[2], v[3]) for v in verticals] + [(s[0], s[1]) for s in sides]
    for on, dev in reach:

        @when(on)
        def _(dev=dev):
            pl.semaphore_signal(
                barrier, inc=1, device_id={"tile": dev}, device_id_type=pl.DeviceIdType.MESH
            )

    loads = [
        (marks_hbm, marks_ref),
        (amount_hbm, amount_ref),
        (adj_hbm, adj_ref),
        (x_hbm, gx.at[0, 0, base:]),
        (v_hbm.at[0], gv.at[0]),
        (k_hbm, k_ref),
        (gain_hbm, gain_ref),
        (w_hbm, w_ref),
        (sharp_hbm, sharp_ref),
        (wo_hbm, wo_ref),
    ]
    loads = [pltpu.make_async_copy(a, b, local.at[i]) for i, (a, b) in enumerate(loads)]
    for load in loads:
        load.start()
    blocks = marks_ref.shape[0]
    per = tok // blocks

    def validity(pos):
        m = jnp.zeros(pos.shape, jnp.int32)
        for b in range(blocks):
            m = jnp.where((pos >= b * per) & (pos < (b + 1) * per), marks_ref[b], m)
        return (m == 1) & (pos < amount_ref[0])

    ri = lax.broadcasted_iota(jnp.int32, (tok, tok), 0)
    ci = lax.broadcasted_iota(jnp.int32, (tok, tok), 1)
    loads[0].wait()
    loads[1].wait()
    loads[2].wait()
    ok = validity(ri)
    up8 = lax.broadcasted_iota(jnp.int32, (16, tok), 0) < 8
    for c, dc in enumerate(COLS):
        up = adj_ref[0, DIRECTIONS.index((-1, dc))]
        down = adj_ref[0, DIRECTIONS.index((1, dc))]
        gx[0, 0, :base, (c + 1) * tok : (c + 2) * tok] = jnp.where(
            jnp.where(up8, up, down) == 1, 1.0, 0.0
        ).astype(jnp.bfloat16)
    gx[0, 0, :base, :tok] = jnp.where(
        validity(lax.broadcasted_iota(jnp.int32, (16, tok), 1)), 1.0, 0.0
    ).astype(jnp.bfloat16)
    e0 = lax.broadcasted_iota(jnp.int32, (qw, qw), 0) >> 6
    e1 = lax.broadcasted_iota(jnp.int32, (qw, qw), 1) >> 6
    ones_s[...] = jnp.where(e0 == e1, 1.0 / hd, 0.0).astype(jnp.bfloat16)

    peers = 0
    for on, dev in reach:
        peers = peers + (1 if on is None else on.astype(jnp.int32))
    pl.semaphore_wait(barrier, peers)

    def start_vertical(s, h):
        for _, there, on, dev in verticals:

            @when(on)
            def _(there=there, dev=dev):
                vcopy(s, h, there, dev).start()

    def start_sides(chunk):
        for side in range(2):

            @when(sides[side][0])
            def _(side=side):
                hcopy(chunk, side).start()

    def unit(u):
        f = u.astype(jnp.float32)
        sq = (f * f).astype(jnp.bfloat16)
        mean = jnp.concatenate(
            [dot(sq[:, i : i + qw], ones_s[...]) for i in range(0, width, qw)], axis=1
        )
        return f * lax.rsqrt(mean + 1e-06)

    loads[3].wait()
    start_vertical(0, 0)
    start_sides(0)
    loads[4].wait()
    start_sides(2)
    loads[5].wait()
    gk[0] = unit(k_ref[0]).astype(jnp.bfloat16)
    start_sides(1)

    for load in loads[6:]:
        load.wait()
    lane = lax.broadcasted_iota(jnp.int32, (1, width), 1)
    scale = jnp.zeros((1, width), jnp.float32)
    for h in range(heads):
        scale = jnp.where(
            (lane >= h * hd) & (lane < (h + 1) * hd), sharp_ref[h] * (LOG2E / hd), scale
        )
    hrow = lax.broadcasted_iota(jnp.int32, (16, width), 0)
    hlane = lax.broadcasted_iota(jnp.int32, (16, width), 1)
    pick = jnp.where(hlane == hrow * hd, 1.0, 0.0).astype(jnp.bfloat16)
    spread = jnp.where(
        (hlane >= hrow * hd) & (hlane < (hrow + 1) * hd), 1.0, 0.0
    ).astype(jnp.bfloat16)
    half = lax.broadcasted_iota(jnp.int32, (ht, 2 * hd), 1) < hd

    for side in range(2):

        @pl.when(jnp.logical_not(sides[side][2]))
        def _(n=1 + side):
            ks[n] = jnp.zeros(ks.shape[1:], jnp.bfloat16)
            vs[n] = jnp.zeros(vs.shape[1:], jnp.bfloat16)
            ms[n] = jnp.zeros(ms.shape[1:], jnp.bfloat16)

    def norm(x):
        f = x.astype(jnp.float32)
        r = lax.rsqrt(jnp.mean(f * f, axis=-1, keepdims=True) + 1e-06)
        return (f * r * gain_ref[...]).astype(jnp.bfloat16)

    lanes = lax.broadcasted_iota(jnp.int32, (ht, qw), 1)

    def make_query(i, h, x):
        u = dot(norm(x), w_ref[:, :width]).astype(jnp.bfloat16)
        query = unit(u) * scale
        for k in range(x.shape[0] // ht):
            for q in range(quads):
                part = query[k * ht : (k + 1) * ht, q * qw : (q + 1) * qw]
                for a in range(4):
                    qs[i, h + k, q, a * ht : (a + 1) * ht, :] = jnp.where(
                        (lanes >= a * hd) & (lanes < (a + 1) * hd), part, 0.0
                    ).astype(jnp.bfloat16)

    def prepare(n):
        line = gx[0, n, :base, :tok].astype(jnp.float32)[:1]
        m = jnp.sum(jnp.where(ri == ci, line, 0.0), axis=1, keepdims=True)
        mb = jnp.broadcast_to(m, (tok, 2 * hd)).astype(jnp.bfloat16)
        ms[n, :tok, :] = mb
        ms[n, tok:, :] = mb
        ks[n, :tok, :] = gk[n]
        vs[n, :tok, :] = (gv[n].astype(jnp.float32) * m).astype(jnp.bfloat16)

    def project(s, n):
        kv = dot(norm(gx[s, n, base:, :]), w_ref[:, width:]).astype(jnp.bfloat16)
        lo = (s + 1) * tok
        ks[n, lo : lo + tok, :] = unit(kv[:, :width]).astype(jnp.bfloat16)
        m = ms[n, :tok, :1].astype(jnp.float32)
        vs[n, lo : lo + tok, :] = (kv[:, width:].astype(jnp.float32) * m).astype(
            jnp.bfloat16
        )

    def attend(s, i, h, seen):
        parts = [attend_quad(s, i, h, q, seen) for q in range(quads)]
        return [jnp.concatenate([p[k] for p in parts], axis=1) for k in range(2)]

    def attend_quad(s, i, h, q, seen):
        sums = [None, None]
        for c in range(3):
            keys = ks[c, s * tok : (s + 2) * tok, q * qw : (q + 1) * qw]
            scores = lax.dot_general(qs[i, h, q], keys, NT, preferred_element_type=jnp.float32)
            p = jnp.exp2(scores).astype(jnp.bfloat16)
            for a in range(2):
                lo = (q * 2 + a) * 2 * hd
                vals = vs[c, s * tok : (s + 2) * tok, lo : lo + 2 * hd]
                r = dot(p[a * 2 * ht : (a + 1) * 2 * ht], jnp.concatenate([vals, ms[c]], axis=1))
                if seen[c] is not None:
                    r = r * seen[c]
                sums[a] = r if sums[a] is None else sums[a] + r
        num, den = [], []
        for r in sums:
            top, bot = r[:ht], r[ht:]
            num.append(jnp.where(half, top[:, : 2 * hd], bot[:, : 2 * hd]))
            den.append(jnp.where(half, top[:, 2 * hd :], bot[:, 2 * hd :]))
        return jnp.concatenate(num, axis=1), jnp.concatenate(den, axis=1)

    own_seen = [None]
    for dc in (-1, 1):
        own_seen.append(jnp.where(adj_ref[0, DIRECTIONS.index((0, dc))] == 1, 1.0, 0.0))

    for s in range(STEPS):
        make_query(0, 0, gx[s, 0, base:, :])
        if s == 0:
            for _, there, on, dev in verticals:

                @when(on)
                def _(there=there, dev=dev):
                    vcopy(0, 0, there, dev).wait_send()
                    vcopy(0, 1, there, dev).start()

            prepare(0)
        project(s, 0)
        for side in range(2):

            @pl.when(sides[side][2])
            def _(side=side):
                for chunk in (0, 2, 1) if s == 0 else (3, 4):
                    hcopy(chunk, side).wait_recv()
                if s == 0:
                    prepare(1 + side)
                project(s, 1 + side)

        for h in range(2):
            for here, there, on, dev in verticals:

                @when(on)
                def _(here=here, there=there, dev=dev):
                    vcopy(s, h, here, dev).wait_recv()
                    lo = base + h * ht
                    make_query(1 + here, h, gx[s, 3 + here, lo : lo + ht, :])
                    lines = gx[0, 3 + here, :base, :].astype(jnp.float32)
                    up, down = lines[:1], lines[8:9]
                    if two:
                        line = jnp.where(row == 0, up, down)
                    else:
                        line = down if here == 0 else up
                    seen = []
                    for c in range(3):
                        part = line[:, (c + 1) * tok : (c + 2) * tok]
                        seen.append(jnp.concatenate([part] * (qw // tok), axis=1))
                    num, den = attend(s, 1 + here, h, seen)
                    psend[s, here, h] = num.astype(jnp.bfloat16)
                    low = lax.dot_general(
                        pick, den.astype(jnp.bfloat16), NT, preferred_element_type=jnp.float32
                    ).astype(jnp.bfloat16)
                    lsend[s, here, h] = jnp.concatenate([low] * 2, axis=1)
                    for copy in pcopies(s, here, there, h, dev):
                        copy.start()

            nums[h], dens[h] = attend(s, 0, h, own_seen)

        for h in range(2):
            for here, _, on, dev in verticals:

                @when(on)
                def _(here=here, dev=dev):
                    for copy in pcopies(s, here, here, h, dev):
                        copy.wait_recv()
                    nums[h] += precv[s, here, h].astype(jnp.float32)
                    dens[h] += lax.dot_general(
                        lrecv[s, here, h],
                        spread,
                        (((0,), (0,)), ((), ())),
                        preferred_element_type=jnp.float32,
                    )[:ht]

            valid = jnp.concatenate([ok[h * ht : (h + 1) * ht]] * (width // tok), axis=1)
            att = jnp.where(valid, nums[h] / jnp.where(valid, dens[h], 1.0), 0.0)
            tend = dot(att.astype(jnp.bfloat16), wo_ref[...]).astype(jnp.bfloat16)
            if s == 0:
                lo = base + h * ht
                x = gx[0, 0, lo : lo + ht, :].astype(jnp.float32)
                gx[1, 0, lo : lo + ht, :] = (x + tend.astype(jnp.float32)).astype(jnp.bfloat16)
                start_vertical(1, h)
                start_sides(3 + h)
            out_ref[s, h * ht : (h + 1) * ht, :] = tend

    for here, there, on, dev in verticals:

        @when(on)
        def _(here=here, there=there, dev=dev):
            for s, h in ((0, 1), (1, 0), (1, 1)):
                vcopy(s, h, there, dev).wait_send()
            for s in range(STEPS):
                for h in range(2):
                    for copy in pcopies(s, here, there, h, dev):
                        copy.wait_send()

    for side in range(2):

        @pl.when(sides[side][0])
        def _(side=side):
            for chunk in range(5):
                hcopy(chunk, side).wait_send()


def body(tiles, x, k, v, gain, w, wo, sharp, adj, marks, amount):
    tok, width = x.shape
    nv = 1 if tiles // TW == 2 else 2
    vmem = pl.BlockSpec(memory_space=pltpu.VMEM)
    hbm = pl.BlockSpec(memory_space=pltpu.HBM)
    bf = jnp.bfloat16
    hd = width // sharp.shape[0]
    qw = 4 * hd
    quads = width // qw
    return pl.pallas_call(
        functools.partial(kernel, tiles),
        out_shape=jax.ShapeDtypeStruct((STEPS, tok, width), bf),
        in_specs=[hbm] * 10,
        out_specs=vmem,
        scratch_shapes=[
            pltpu.VMEM(k.shape, bf),
            pltpu.VMEM((1, width), jnp.float32),
            pltpu.VMEM(w.shape, bf),
            pltpu.VMEM(wo.shape, bf),
            pltpu.SMEM(sharp.shape, jnp.float32),
            pltpu.SMEM(adj.shape, jnp.int32),
            pltpu.SMEM(marks.shape, jnp.int32),
            pltpu.SMEM(amount.shape, jnp.int32),
            pltpu.SemaphoreType.DMA((10,)),
            pltpu.VMEM((STEPS, 3 + nv, tok + 16, width), bf),
            pltpu.VMEM((3, tok, width), bf),
            pltpu.VMEM((3, tok, width), bf),
            pltpu.VMEM((3, 3 * tok, width), bf),
            pltpu.VMEM((3, 3 * tok, width), bf),
            pltpu.VMEM((3, 2 * tok, 2 * hd), bf),
            pltpu.VMEM((1 + nv, 2, quads, 2 * tok, qw), bf),
            pltpu.VMEM((2, tok // 2, width), jnp.float32),
            pltpu.VMEM((2, tok // 2, width), jnp.float32),
            pltpu.VMEM((STEPS, nv, 2, tok // 2, width), bf),
            pltpu.VMEM((STEPS, nv, 2, tok // 2, width), bf),
            pltpu.VMEM((STEPS, nv, 2, 16, tok), bf),
            pltpu.VMEM((STEPS, nv, 2, 16, tok), bf),
            pltpu.VMEM((qw, qw), bf),
            pltpu.SemaphoreType.DMA((STEPS, 2, nv)),
            pltpu.SemaphoreType.DMA((STEPS, 2, nv)),
            pltpu.SemaphoreType.DMA((5, 2)),
            pltpu.SemaphoreType.DMA((5, 2)),
            pltpu.SemaphoreType.DMA((STEPS, nv, 4)),
            pltpu.SemaphoreType.DMA((STEPS, nv, 4)),
        ],
        compiler_params=pltpu.CompilerParams(
            collective_id=0, has_side_effects=True, vmem_limit_bytes=62 * 1024 * 1024
        ),
    )(x, k, v, gain.reshape(1, width), w, wo, sharp, adj, marks, amount)


def solution(mesh):
    part = ("grp", "tile")
    in_specs = (
        P(part, None),
        P(None, part, None),
        P(None, part, None),
        P(),
        P(),
        P(),
        P(),
        P(part, None),
        P(part),
        P(part),
    )
    return jax.shard_map(
        functools.partial(body, mesh.shape["tile"]),
        mesh=mesh,
        in_specs=in_specs,
        out_specs=P(None, part, None),
        check_vma=False,
    )
```

```python
import functools

import jax
import jax.numpy as jnp
from jax import lax
from jax.experimental import pallas as pl
from jax.experimental.pallas import tpu as pltpu
from jax.sharding import PartitionSpec as P

TW = 8
STEPS = 2
COLS = (0, -1, 1)
LOG2E = 1.4426950408889634
NT = (((1,), (1,)), ((), ()))
DIRECTIONS = ((-1, -1), (-1, 0), (-1, 1), (0, -1), (0, 1), (1, -1), (1, 0), (1, 1))


def dot(a, b):
    return jnp.dot(a, b, preferred_element_type=jnp.float32)


def kernel(
    tiles,
    x_hbm,
    k_hbm,
    v_hbm,
    gain_hbm,
    w_hbm,
    wo_hbm,
    sharp_hbm,
    adj_hbm,
    marks_hbm,
    amount_hbm,
    out_ref,
    gain_ref,
    w_ref,
    wo_ref,
    sharp_ref,
    adj_ref,
    marks_ref,
    amount_ref,
    local,
    gx,
    gk,
    gv,
    ks,
    vs,
    ms,
    qs,
    nums,
    dens,
    psend,
    precv,
    lsend,
    lrecv,
    ones_s,
    send_v,
    recv_v,
    send_h,
    recv_h,
    send_p,
    recv_p,
):
    tok, width = x_hbm.shape
    heads = sharp_hbm.shape[0]
    hd = width // heads
    qw = 4 * hd
    quads = width // qw
    ht = tok // 2
    base = 16
    rows = tiles // TW
    t = lax.axis_index("tile")
    row = t // TW
    col = t % TW
    two = rows == 2
    has_left = col > 0
    has_right = col < TW - 1
    if two:
        verticals = [(0, 0, None, jnp.where(row == 0, t + TW, t - TW))]
    else:
        verticals = [
            (0, 1, row > 0, jnp.maximum(t - TW, 0)),
            (1, 0, row < rows - 1, jnp.minimum(t + TW, tiles - 1)),
        ]
    sides = [
        (has_right, jnp.minimum(t + 1, tiles - 1), has_left),
        (has_left, jnp.maximum(t - 1, 0), has_right),
    ]

    def when(cond):
        return (lambda f: f()) if cond is None else pl.when(cond)

    def place(chunk, slot):
        if chunk == 0:
            return gx.at[0, slot]
        if chunk >= 3:
            lo = base + (chunk - 3) * ht
            return gx.at[1, slot, lo : lo + ht]
        return (gk if chunk == 1 else gv).at[slot]

    def remote(src, dst, send, recv, dev):
        return pltpu.make_async_remote_copy(
            src_ref=src,
            dst_ref=dst,
            send_sem=send,
            recv_sem=recv,
            device_id={"tile": dev},
            device_id_type=pl.DeviceIdType.MESH,
        )

    def vcopy(s, h, at, dev):
        lo = 0 if s == 0 and h == 0 else base + h * ht
        hi = base + (h + 1) * ht
        return remote(
            gx.at[s, 0, lo:hi],
            gx.at[s, 3 + at, lo:hi],
            send_v.at[s, h, at],
            recv_v.at[s, h, at],
            dev,
        )

    def hcopy(chunk, side):
        return remote(
            place(chunk, 0),
            place(chunk, 1 + side),
            send_h.at[chunk, side],
            recv_h.at[chunk, side],
            sides[side][1],
        )

    def pcopies(s, src, dst, h, dev):
        return [
            remote(a.at[s, src, h], b.at[s, dst, h], send_p.at[s, dst, k], recv_p.at[s, dst, k], dev)
            for k, a, b in ((2 * h, lsend, lrecv), (2 * h + 1, psend, precv))
        ]

    barrier = pltpu.get_barrier_semaphore()
    reach = [(v[2], v[3]) for v in verticals] + [(s[0], s[1]) for s in sides]
    for on, dev in reach:

        @when(on)
        def _(dev=dev):
            pl.semaphore_signal(
                barrier, inc=1, device_id={"tile": dev}, device_id_type=pl.DeviceIdType.MESH
            )

    loads = [
        (marks_hbm, marks_ref),
        (amount_hbm, amount_ref),
        (adj_hbm, adj_ref),
        (x_hbm, gx.at[0, 0, base:]),
        (v_hbm.at[0], gv.at[0]),
        (k_hbm.at[0], gk.at[0]),
        (gain_hbm, gain_ref),
        (w_hbm, w_ref),
        (sharp_hbm, sharp_ref),
        (wo_hbm, wo_ref),
    ]
    loads = [pltpu.make_async_copy(a, b, local.at[i]) for i, (a, b) in enumerate(loads)]
    for load in loads:
        load.start()
    blocks = marks_ref.shape[0]
    per = tok // blocks

    def validity(pos):
        m = jnp.zeros(pos.shape, jnp.int32)
        for b in range(blocks):
            m = jnp.where((pos >= b * per) & (pos < (b + 1) * per), marks_ref[b], m)
        return (m == 1) & (pos < amount_ref[0])

    ri = lax.broadcasted_iota(jnp.int32, (tok, tok), 0)
    ci = lax.broadcasted_iota(jnp.int32, (tok, tok), 1)
    loads[0].wait()
    loads[1].wait()
    loads[2].wait()
    ok = validity(ri)
    up8 = lax.broadcasted_iota(jnp.int32, (16, tok), 0) < 8
    for c, dc in enumerate(COLS):
        up = adj_ref[0, DIRECTIONS.index((-1, dc))]
        down = adj_ref[0, DIRECTIONS.index((1, dc))]
        gx[0, 0, :base, (c + 1) * tok : (c + 2) * tok] = jnp.where(
            jnp.where(up8, up, down) == 1, 1.0, 0.0
        ).astype(jnp.bfloat16)
    gx[0, 0, :base, :tok] = jnp.where(
        validity(lax.broadcasted_iota(jnp.int32, (16, tok), 1)), 1.0, 0.0
    ).astype(jnp.bfloat16)
    e0 = lax.broadcasted_iota(jnp.int32, (qw, qw), 0) >> 6
    e1 = lax.broadcasted_iota(jnp.int32, (qw, qw), 1) >> 6
    ones_s[...] = jnp.where(e0 == e1, 1.0 / hd, 0.0).astype(jnp.bfloat16)

    peers = 0
    for on, dev in reach:
        peers = peers + (1 if on is None else on.astype(jnp.int32))
    pl.semaphore_wait(barrier, peers)

    def start_vertical(s, h):
        for _, there, on, dev in verticals:

            @when(on)
            def _(there=there, dev=dev):
                vcopy(s, h, there, dev).start()

    def start_sides(chunk):
        for side in range(2):

            @when(sides[side][0])
            def _(side=side):
                hcopy(chunk, side).start()

    def unit(u):
        f = u.astype(jnp.float32)
        sq = (f * f).astype(jnp.bfloat16)
        mean = jnp.concatenate(
            [dot(sq[:, i : i + qw], ones_s[...]) for i in range(0, width, qw)], axis=1
        )
        return f * lax.rsqrt(mean + 1e-06)

    loads[3].wait()
    start_vertical(0, 0)
    start_sides(0)
    loads[4].wait()
    start_sides(2)
    loads[5].wait()
    start_sides(1)

    for load in loads[6:]:
        load.wait()
    lane = lax.broadcasted_iota(jnp.int32, (1, width), 1)
    scale = jnp.zeros((1, width), jnp.float32)
    for h in range(heads):
        scale = jnp.where(
            (lane >= h * hd) & (lane < (h + 1) * hd), sharp_ref[h] * (LOG2E / hd), scale
        )
    hrow = lax.broadcasted_iota(jnp.int32, (16, width), 0)
    hlane = lax.broadcasted_iota(jnp.int32, (16, width), 1)
    pick = jnp.where(hlane == hrow * hd, 1.0, 0.0).astype(jnp.bfloat16)
    spread = jnp.where(
        (hlane >= hrow * hd) & (hlane < (hrow + 1) * hd), 1.0, 0.0
    ).astype(jnp.bfloat16)
    half = lax.broadcasted_iota(jnp.int32, (ht, 2 * hd), 1) < hd

    for side in range(2):

        @pl.when(jnp.logical_not(sides[side][2]))
        def _(n=1 + side):
            ks[n] = jnp.zeros(ks.shape[1:], jnp.bfloat16)
            vs[n] = jnp.zeros(vs.shape[1:], jnp.bfloat16)
            ms[n] = jnp.zeros(ms.shape[1:], jnp.bfloat16)

    def norm(x):
        f = x.astype(jnp.float32)
        r = lax.rsqrt(jnp.mean(f * f, axis=-1, keepdims=True) + 1e-06)
        return (f * r * gain_ref[...]).astype(jnp.bfloat16)

    lanes = lax.broadcasted_iota(jnp.int32, (ht, qw), 1)

    def make_query(i, h, x):
        u = dot(norm(x), w_ref[:, :width]).astype(jnp.bfloat16)
        query = unit(u) * scale
        for k in range(x.shape[0] // ht):
            for q in range(quads):
                part = query[k * ht : (k + 1) * ht, q * qw : (q + 1) * qw]
                for a in range(4):
                    qs[i, h + k, q, a * ht : (a + 1) * ht, :] = jnp.where(
                        (lanes >= a * hd) & (lanes < (a + 1) * hd), part, 0.0
                    ).astype(jnp.bfloat16)

    def prepare(n):
        line = gx[0, n, :base, :tok].astype(jnp.float32)[:1]
        m = jnp.sum(jnp.where(ri == ci, line, 0.0), axis=1, keepdims=True)
        mb = jnp.broadcast_to(m, (tok, 2 * hd)).astype(jnp.bfloat16)
        ms[n, :tok, :] = mb
        ms[n, tok:, :] = mb
        ks[n, :tok, :] = unit(gk[n]).astype(jnp.bfloat16)
        vs[n, :tok, :] = (gv[n].astype(jnp.float32) * m).astype(jnp.bfloat16)

    def project(s, n):
        kv = dot(norm(gx[s, n, base:, :]), w_ref[:, width:]).astype(jnp.bfloat16)
        lo = (s + 1) * tok
        ks[n, lo : lo + tok, :] = unit(kv[:, :width]).astype(jnp.bfloat16)
        m = ms[n, :tok, :1].astype(jnp.float32)
        vs[n, lo : lo + tok, :] = (kv[:, width:].astype(jnp.float32) * m).astype(
            jnp.bfloat16
        )

    def attend(s, i, h, seen):
        parts = [attend_quad(s, i, h, q, seen) for q in range(quads)]
        return [jnp.concatenate([p[k] for p in parts], axis=1) for k in range(2)]

    def attend_quad(s, i, h, q, seen):
        sums = [None, None]
        for c in range(3):
            keys = ks[c, s * tok : (s + 2) * tok, q * qw : (q + 1) * qw]
            scores = lax.dot_general(qs[i, h, q], keys, NT, preferred_element_type=jnp.float32)
            p = jnp.exp2(scores).astype(jnp.bfloat16)
            for a in range(2):
                lo = (q * 2 + a) * 2 * hd
                vals = vs[c, s * tok : (s + 2) * tok, lo : lo + 2 * hd]
                r = dot(p[a * 2 * ht : (a + 1) * 2 * ht], jnp.concatenate([vals, ms[c]], axis=1))
                if seen[c] is not None:
                    r = r * seen[c]
                sums[a] = r if sums[a] is None else sums[a] + r
        num, den = [], []
        for r in sums:
            top, bot = r[:ht], r[ht:]
            num.append(jnp.where(half, top[:, : 2 * hd], bot[:, : 2 * hd]))
            den.append(jnp.where(half, top[:, 2 * hd :], bot[:, 2 * hd :]))
        return jnp.concatenate(num, axis=1), jnp.concatenate(den, axis=1)

    own_seen = [None]
    for dc in (-1, 1):
        own_seen.append(jnp.where(adj_ref[0, DIRECTIONS.index((0, dc))] == 1, 1.0, 0.0))

    for s in range(STEPS):
        make_query(0, 0, gx[s, 0, base:, :])
        if s == 0:
            for _, there, on, dev in verticals:

                @when(on)
                def _(there=there, dev=dev):
                    vcopy(0, 1, there, dev).start()

            prepare(0)
        project(s, 0)
        for side in range(2):

            @pl.when(sides[side][2])
            def _(side=side):
                for chunk in (0, 2, 1) if s == 0 else (3, 4):
                    hcopy(chunk, side).wait_recv()
                if s == 0:
                    prepare(1 + side)
                project(s, 1 + side)

        for h in range(2):
            for here, there, on, dev in verticals:

                @when(on)
                def _(here=here, there=there, dev=dev):
                    vcopy(s, h, here, dev).wait_recv()
                    lo = base + h * ht
                    make_query(1 + here, h, gx[s, 3 + here, lo : lo + ht, :])
                    lines = gx[0, 3 + here, :base, :].astype(jnp.float32)
                    up, down = lines[:1], lines[8:9]
                    if two:
                        line = jnp.where(row == 0, up, down)
                    else:
                        line = down if here == 0 else up
                    seen = []
                    for c in range(3):
                        part = line[:, (c + 1) * tok : (c + 2) * tok]
                        seen.append(jnp.concatenate([part] * (qw // tok), axis=1))
                    num, den = attend(s, 1 + here, h, seen)
                    psend[s, here, h] = num.astype(jnp.bfloat16)
                    low = lax.dot_general(
                        pick, den.astype(jnp.bfloat16), NT, preferred_element_type=jnp.float32
                    ).astype(jnp.bfloat16)
                    lsend[s, here, h] = jnp.concatenate([low] * 2, axis=1)
                    for copy in pcopies(s, here, there, h, dev):
                        copy.start()

            nums[h], dens[h] = attend(s, 0, h, own_seen)

        for h in range(2):
            for here, _, on, dev in verticals:

                @when(on)
                def _(here=here, dev=dev):
                    for copy in pcopies(s, here, here, h, dev):
                        copy.wait_recv()
                    nums[h] += precv[s, here, h].astype(jnp.float32)
                    dens[h] += lax.dot_general(
                        lrecv[s, here, h],
                        spread,
                        (((0,), (0,)), ((), ())),
                        preferred_element_type=jnp.float32,
                    )[:ht]

            valid = jnp.concatenate([ok[h * ht : (h + 1) * ht]] * (width // tok), axis=1)
            att = jnp.where(valid, nums[h] / jnp.where(valid, dens[h], 1.0), 0.0)
            tend = dot(att.astype(jnp.bfloat16), wo_ref[...]).astype(jnp.bfloat16)
            if s == 0:
                lo = base + h * ht
                x = gx[0, 0, lo : lo + ht, :].astype(jnp.float32)
                gx[1, 0, lo : lo + ht, :] = (x + tend.astype(jnp.float32)).astype(jnp.bfloat16)
                start_vertical(1, h)
                start_sides(3 + h)
            out_ref[s, h * ht : (h + 1) * ht, :] = tend

    for here, there, on, dev in verticals:

        @when(on)
        def _(here=here, there=there, dev=dev):
            for s, h in ((0, 0), (0, 1), (1, 0), (1, 1)):
                vcopy(s, h, there, dev).wait_send()
            for s in range(STEPS):
                for h in range(2):
                    for copy in pcopies(s, here, there, h, dev):
                        copy.wait_send()

    for side in range(2):

        @pl.when(sides[side][0])
        def _(side=side):
            for chunk in range(5):
                hcopy(chunk, side).wait_send()


def body(tiles, x, k, v, gain, w, wo, sharp, adj, marks, amount):
    tok, width = x.shape
    nv = 1 if tiles // TW == 2 else 2
    vmem = pl.BlockSpec(memory_space=pltpu.VMEM)
    hbm = pl.BlockSpec(memory_space=pltpu.HBM)
    bf = jnp.bfloat16
    hd = width // sharp.shape[0]
    qw = 4 * hd
    quads = width // qw
    return pl.pallas_call(
        functools.partial(kernel, tiles),
        out_shape=jax.ShapeDtypeStruct((STEPS, tok, width), bf),
        in_specs=[hbm] * 10,
        out_specs=vmem,
        scratch_shapes=[
            pltpu.VMEM((1, width), jnp.float32),
            pltpu.VMEM(w.shape, bf),
            pltpu.VMEM(wo.shape, bf),
            pltpu.SMEM(sharp.shape, jnp.float32),
            pltpu.SMEM(adj.shape, jnp.int32),
            pltpu.SMEM(marks.shape, jnp.int32),
            pltpu.SMEM(amount.shape, jnp.int32),
            pltpu.SemaphoreType.DMA((10,)),
            pltpu.VMEM((STEPS, 3 + nv, tok + 16, width), bf),
            pltpu.VMEM((3, tok, width), bf),
            pltpu.VMEM((3, tok, width), bf),
            pltpu.VMEM((3, 3 * tok, width), bf),
            pltpu.VMEM((3, 3 * tok, width), bf),
            pltpu.VMEM((3, 2 * tok, 2 * hd), bf),
            pltpu.VMEM((1 + nv, 2, quads, 2 * tok, qw), bf),
            pltpu.VMEM((2, tok // 2, width), jnp.float32),
            pltpu.VMEM((2, tok // 2, width), jnp.float32),
            pltpu.VMEM((STEPS, nv, 2, tok // 2, width), bf),
            pltpu.VMEM((STEPS, nv, 2, tok // 2, width), bf),
            pltpu.VMEM((STEPS, nv, 2, 16, tok), bf),
            pltpu.VMEM((STEPS, nv, 2, 16, tok), bf),
            pltpu.VMEM((qw, qw), bf),
            pltpu.SemaphoreType.DMA((STEPS, 2, nv)),
            pltpu.SemaphoreType.DMA((STEPS, 2, nv)),
            pltpu.SemaphoreType.DMA((5, 2)),
            pltpu.SemaphoreType.DMA((5, 2)),
            pltpu.SemaphoreType.DMA((STEPS, nv, 4)),
            pltpu.SemaphoreType.DMA((STEPS, nv, 4)),
        ],
        compiler_params=pltpu.CompilerParams(
            collective_id=0, has_side_effects=True, vmem_limit_bytes=62 * 1024 * 1024
        ),
    )(x, k, v, gain.reshape(1, width), w, wo, sharp, adj, marks, amount)


def solution(mesh):
    part = ("grp", "tile")
    in_specs = (
        P(part, None),
        P(None, part, None),
        P(None, part, None),
        P(),
        P(),
        P(),
        P(),
        P(part, None),
        P(part),
        P(part),
    )
    return jax.shard_map(
        functools.partial(body, mesh.shape["tile"]),
        mesh=mesh,
        in_specs=in_specs,
        out_specs=P(None, part, None),
        check_vma=False,
    )
```
